32 devices in a mesh: expert: 4 (over y, x), tensor: 8 (over z, core).
Axes of the slice: x: 2, y: 2, z: 4, core: 2. Of those that a mesh axis runs over, the one named last changes fastest.
Arguments:
- tokens: bfloat16 [512, 6144], P('expert'), may hold values from -6 to 6
- routes: int32 [512, 4], P('expert'), may hold values from 0 to 15, all different within a row; in each aligned block of 128 rows (0 to 127, 128 to 255, ...) at most 40 rows name the same one
- gates: float32 [512, 4], P('expert'), may hold values from 0.05 to 1
- gate_proj: bfloat16 [4, 10752, 6144], P('expert', 'tensor'), may hold values from -0.078125 to 0.078125
- up_proj: bfloat16 [4, 10752, 6144], P('expert', 'tensor'), may hold values from -0.078125 to 0.078125
- down_proj: bfloat16 [4, 6144, 10752], P('expert', 'tensor'), may hold values from -0.0625 to 0.0625
Outputs:
- combined: bfloat16 [512, 6144], P('expert', 'tensor')
The draws below stay inside these ranges and needn't reach their ends.
Inputs may be any that keep to these rules, and one draw needn't show every extreme that they name: `routes`: the ids of one row are distinct. In each aligned block of 128 rows no id is named by more than 40 rows, a bound that some block reaches.
All inputs are finite; a program needn't handle non-finite values.
Results may differ from the reference program's by a relative error of at most 0.0057.
Values may be sent and summed in bfloat16 or wider, within the bound.
A program may use at most 128 MiB of HBM per device.

```python
import math
import jax
import jax.numpy as jnp
import numpy as np
from jax import lax

D = 6144
FF = 10752
EXPERTS = 16
TOP = 4
WIN = 4
ROWS_DEV = 128
CAP = 40
FF_G = 10752
GROUPS = 4
ROWS = 512


def steps_of(key, dims, cuts, low, largest):
    gain, own = 1.0, jax.random.fold_in(key, 6)
    for dim, blocks in cuts:
        steps = jnp.exp(jax.random.uniform(jax.random.fold_in(own, dim), (blocks,), jnp.float32, low / len(cuts), largest / len(cuts)))
        gain = gain * jnp.repeat(steps, dims[dim] // blocks).reshape([-1 if axis == dim else 1 for axis in range(len(dims))])
    return gain


def shared_out(own_key, own, number, rows, count, top, most, slope):
    sequence = jax.random.permutation(own_key, count)
    crowded, common = shares(count, rows * top, most, slope, True), shares(count, rows * top, most, slope, False)
    places = jnp.arange(count)

    def named(lengths, rotation):
        used = int((lengths > 0).sum())
        fixed = max(1, used // 4)
        shifted = fixed + (places - fixed + rotation * (used - fixed)) % max(1, count - fixed)
        return jnp.zeros((count,), jnp.int32).at[sequence[jnp.where(places < fixed, places, shifted)]].set(jnp.asarray(lengths, jnp.int32))

    lengths = jnp.where(number % 4 == 0, named(crowded, number // 4), named(common, number - number // 4 - 1))
    mixed = jax.random.permutation(jax.random.fold_in(own, 3), count)
    giver, receiver = mixed[0:count // 2 * 2:2], mixed[1:count // 2 * 2:2]
    slack = jnp.minimum(lengths[giver] - 1, most - lengths[receiver]) // 2
    slack = jnp.where((giver == sequence[0]) | (receiver == sequence[0]) | (lengths[receiver] == 0), 0, jnp.maximum(slack, 0))
    shifted = jax.random.randint(jax.random.fold_in(own, 4), (count // 2,), 0, 1 << 20) % (slack + 1)
    lengths = lengths.at[giver].add(-shifted).at[receiver].add(shifted)
    labels = jnp.searchsorted(jnp.cumsum(lengths), jnp.arange(rows * top), side="right").astype(jnp.int32)
    table = labels.reshape(top, rows).T
    table = table[jax.random.permutation(jax.random.fold_in(own, 1), rows)]
    rotation = jax.random.randint(jax.random.fold_in(own, 2), (rows, 1), 0, top)
    return jnp.take_along_axis(table, (jnp.arange(top)[None, :] + rotation) % top, axis=1)


def shares(count, total, bound, lean, full):
    portions = [(1 << 20) // math.isqrt(grade ** lean) + 1 for grade in range(1, count + 1)]
    largest = bound if full else min(bound, max(-(-total // count), total * portions[0] // sum(portions)))
    least = 1 if total - largest >= count - 1 else 0
    given, spare = [largest] + [least] * (count - 1), total - largest - least * (count - 1)
    while spare > 0:
        movable = [i for i in range(1, count) if given[i] < largest] or [i for i in range(1, count) if given[i] < bound]
        pool, budget = sum([portions[i] for i in movable]), spare
        for i in movable:
            addition = min(bound - given[i], max(1, budget * portions[i] // pool), spare)
            given[i] = given[i] + addition
            spare = spare - addition
    return np.array(given)


def bell_draw(rng, dims, spread, bound, pieces=(), kind=jnp.bfloat16):
    entries = spread * jax.random.normal(rng, dims, jnp.float32)
    if pieces:
        entries = entries * steps_of(rng, dims, pieces, -0.22, 0.18)
    return jnp.clip(entries, -bound, bound).astype(kind)


def setup_inputs(seed: int = 0) -> dict:
    streams_of = jax.random.split(jax.random.key(seed), 7)
    tokens = bell_draw(streams_of[0], (ROWS, D), 1.0, 6.0, ((0, 4),))
    routes_keys = jax.random.split(jax.random.fold_in(streams_of[1], 1), ROWS // ROWS_DEV)
    routes_turns = jax.random.permutation(jax.random.fold_in(streams_of[1], 3), ROWS // ROWS_DEV)
    routes = jax.vmap(lambda own, number: shared_out(jax.random.fold_in(streams_of[1], 2), own, number, ROWS_DEV, EXPERTS, TOP, CAP, 2))(routes_keys, routes_turns).reshape((ROWS, TOP))
    gates = jnp.clip(jnp.exp(math.log(1.0) - 2.9957323 * jax.random.uniform(streams_of[2], (ROWS, TOP), jnp.float32) ** steps_of(streams_of[2], (ROWS, TOP), ((0, 4),), -0.2, 0.2)), 0.05, 1.0)
    gate_proj = bell_draw(streams_of[3], (GROUPS, FF_G, D), D ** -0.5, 0.078125, ((0, 4), (1, 8)))
    up_proj = bell_draw(streams_of[4], (GROUPS, FF_G, D), D ** -0.5, 0.078125, ((0, 4), (1, 8)))
    down_proj = bell_draw(streams_of[5], (GROUPS, D, FF_G), FF ** -0.5, 0.0625, ((0, 4), (1, 8)))
    return {"tokens": tokens, "routes": routes, "gates": gates, "gate_proj": gate_proj, "up_proj": up_proj, "down_proj": down_proj}


def slot_tables(route_block, gate_block):
    row_count = route_block.shape[0]
    experts = jnp.arange(WIN, dtype=jnp.int32)
    hits = route_block[None, :, :] == experts[:, None, None]
    chosen = jnp.any(hits, axis=2)
    position = (jnp.cumsum(chosen.astype(jnp.int32), axis=1) - 1).astype(jnp.int32)
    slots = jnp.arange(CAP, dtype=jnp.int32)
    match = chosen[:, None, :] & (position[:, None, :] == slots[None, :, None])
    row_ids = jnp.arange(row_count, dtype=jnp.int32)
    row_index = jnp.sum(jnp.where(match, row_ids[None, None, :], 0), axis=2).astype(jnp.int32)
    filled = jnp.any(match, axis=2)
    weight = jnp.sum(jnp.where(hits, gate_block[None, :, :], jnp.zeros((), gate_block.dtype)), axis=2)
    return position, row_index, filled, weight


def reference(tokens, routes, gates, gate_proj, up_proj, down_proj):
    groups = gate_proj.shape[0]
    split = groups // WIN
    token_blocks = tokens.reshape(groups, ROWS_DEV, D)
    route_blocks = routes.reshape(groups, ROWS_DEV, TOP)
    gate_blocks = gates.reshape(groups, ROWS_DEV, TOP)
    position, row_index, filled, weight = jax.vmap(slot_tables)(route_blocks, gate_blocks)
    picked = jax.vmap(lambda block, index: jnp.take(block, index, axis=0))(token_blocks, row_index)
    picked = jnp.where(filled[..., None], picked, jnp.zeros((), tokens.dtype))
    per_expert = jnp.transpose(picked, (1, 0, 2, 3)).reshape(WIN, groups * CAP, D)

    def expert_group(group):
        dispatched = per_expert[group // split]
        gate_act = jnp.dot(dispatched, gate_proj[group].T, preferred_element_type=jnp.float32)
        up_act = jnp.dot(dispatched, up_proj[group].T, preferred_element_type=jnp.float32)
        hidden = (jax.nn.silu(gate_act) * up_act).astype(jnp.bfloat16)
        return jnp.dot(hidden, down_proj[group].T, preferred_element_type=jnp.float32).astype(jnp.bfloat16)

    partial_value = lax.map(expert_group, jnp.arange(groups, dtype=jnp.int32))
    expert_out = partial_value.astype(jnp.float32).reshape(WIN, split, groups, CAP, D).sum(axis=1)
    expert_out = jnp.transpose(expert_out, (1, 0, 2, 3))

    def combine(block_sum, block_position, block_weight):
        flat_sum = block_sum.reshape(WIN * CAP, D)
        offsets = jnp.arange(WIN, dtype=jnp.int32)[:, None] * CAP
        index = (offsets + jnp.clip(block_position, 0, CAP - 1)).astype(jnp.int32)
        values = jnp.take(flat_sum, index, axis=0)
        return jnp.sum(values * block_weight[..., None], axis=0)

    combined = jax.vmap(combine)(expert_out, position, weight)
    return combined.reshape(ROWS, D).astype(jnp.bfloat16)
```

```python
import functools
import jax
import jax.numpy as jnp
from jax import lax
from jax.experimental import pallas as pl
from jax.experimental.pallas import tpu as pltpu
from jax.sharding import PartitionSpec as P

WIN = 4
CAP = 40
MESH = pl.DeviceIdType.MESH


def slot_tables(route_block, gate_block):
    row_count = route_block.shape[0]
    experts = jnp.arange(WIN, dtype=jnp.int32)
    hits = route_block[None, :, :] == experts[:, None, None]
    chosen = jnp.any(hits, axis=2)
    position = jnp.cumsum(chosen.astype(jnp.int32), axis=1) - 1
    slots = jnp.arange(CAP, dtype=jnp.int32)
    match = chosen[:, None, :] & (position[:, None, :] == slots[None, :, None])
    row_ids = jnp.arange(row_count, dtype=jnp.int32)
    row_index = jnp.sum(jnp.where(match, row_ids[None, None, :], 0), axis=2)
    filled = jnp.any(match, axis=2)
    weight = jnp.sum(
        jnp.where(hits, gate_block[None, :, :], jnp.zeros((), gate_block.dtype)), axis=2
    )
    return (position, row_index, filled, weight)


def contract_last(left, right):
    return lax.dot_general(
        left, right, (((1,), (1,)), ((), ())), preferred_element_type=jnp.float32
    )


def plain_body(tokens, routes, gates, gate_proj, up_proj, down_proj):
    groups = lax.axis_size("expert")
    split = groups // WIN
    width = tokens.shape[1]
    w_gate = gate_proj[0]
    w_up = up_proj[0]
    w_down = down_proj[0]
    position, row_index, filled, weight = slot_tables(routes, gates)
    picked = jnp.take(tokens, row_index, axis=0)
    picked = jnp.where(filled[:, :, None], picked, jnp.zeros((), tokens.dtype))
    outgoing = jnp.repeat(picked, split, axis=0)
    slot_rows = groups * CAP
    arrived = lax.all_to_all(outgoing, "expert", split_axis=0, concat_axis=0, tiled=True)
    flat_rows = arrived.reshape(slot_rows, width)
    gate_act = contract_last(flat_rows, w_gate)
    up_act = contract_last(flat_rows, w_up)
    hidden = (jax.nn.silu(gate_act) * up_act).astype(jnp.bfloat16)
    partial_value = contract_last(lax.all_gather(hidden, "tensor", axis=1, tiled=True), w_down)
    partial_value = partial_value.astype(jnp.bfloat16).reshape(groups, CAP, w_down.shape[0])
    returned = lax.all_to_all(partial_value, "expert", split_axis=0, concat_axis=0, tiled=True)
    expert_out = returned.astype(jnp.float32).reshape(WIN, split, CAP, w_down.shape[0]).sum(axis=1)
    flat_sum = expert_out.reshape(WIN * CAP, w_down.shape[0])
    offsets = jnp.arange(WIN, dtype=jnp.int32)[:, None] * CAP
    index = offsets + jnp.clip(position, 0, CAP - 1)
    values = jnp.take(flat_sum, index, axis=0)
    return jnp.sum(values * weight[:, :, None], axis=0).astype(jnp.bfloat16)


CUTS = (0, 32, 112, 160)
CHUNK = 256


def kernel(cfg, tok_h, rou_h, gat_h, wg_h, wu_h, wd_h, out_ref,
           tok, rou, gat, wg, wu, wd, sbuf, xr, xa, xb, xc, hid, carry, acc, pbuf, ret, wmat,
           in_sem, w_sem, d_sem, ds_send, ds_recv, fw_send, fw_recv,
           up_send, dn_send, sb_send, ag_recv, rt_send, rt_recv):
    depth, units, feats, rows = cfg
    chips = 4
    quarter = depth // 4
    pad_units = wg.shape[0]
    half_pad = pad_units - units
    me = lax.axis_index("expert")
    t = lax.axis_index("tensor")
    z = t // 2
    c = t % 2
    x = me % 2
    y = me // 2
    sib = t + 1 - 2 * c
    rel = [me, y * 2 + (1 - x), (1 - y) * 2 + x, (1 - y) * 2 + (1 - x)]

    small = [pltpu.make_async_copy(rou_h, rou, in_sem.at[0]),
             pltpu.make_async_copy(gat_h, gat, in_sem.at[1]),
             pltpu.make_async_copy(tok_h, tok, in_sem.at[2])]
    for copy in small:
        copy.start()
    spans = [(k, min(CHUNK, units - k)) for k in range(0, units, CHUNK)]
    loads = []
    for k, (start, size) in enumerate(spans):
        dst = pl.multiple_of(start + half_pad * c, half_pad)
        loads.append([
            pltpu.make_async_copy(wg_h.at[0, pl.ds(start, size), :], wg.at[pl.ds(dst, size), :], w_sem.at[0, k]),
            pltpu.make_async_copy(wu_h.at[0, pl.ds(start, size), :], wu.at[pl.ds(dst, size), :], w_sem.at[1, k])])
    for pair in loads:
        for copy in pair:
            copy.start()
    wd_load = pltpu.make_async_copy(wd_h.at[0], wd, d_sem)
    wd_load.start()
    gap = pl.multiple_of((1 - c) * units, half_pad)
    wg[pl.ds(gap, half_pad), :] = jnp.zeros((half_pad, depth), wg.dtype)
    wu[pl.ds(gap, half_pad), :] = jnp.zeros((half_pad, depth), wu.dtype)

    barrier = pltpu.get_barrier_semaphore()
    for r in (1, 2, 3):
        pl.semaphore_signal(barrier, inc=1, device_id=(rel[r], t), device_id_type=MESH)
    pl.semaphore_signal(barrier, inc=1, device_id=(me, sib), device_id_type=MESH)

    @pl.when(z < chips - 1)
    def _():
        pl.semaphore_signal(barrier, inc=1, device_id=(me, t + 2), device_id_type=MESH)

    @pl.when(z > 0)
    def _():
        pl.semaphore_signal(barrier, inc=1, device_id=(me, t - 2), device_id_type=MESH)

    small[0].wait()
    small[1].wait()
    lane = lax.broadcasted_iota(jnp.int32, (rows, 256), 1)
    group = (lane >= CAP).astype(jnp.int32) + (lane >= 2 * CAP).astype(jnp.int32) + (lane >= 3 * CAP).astype(jnp.int32)
    named = jnp.where(group == 0, rel[0], jnp.where(group == 1, rel[1], jnp.where(group == 2, rel[2], rel[3])))
    named = jnp.where(lane >= 4 * CAP, -1, named)
    slot = lane - CAP * group
    routes = rou[...]
    gates = gat[...]
    chosen = jnp.zeros((rows, 256), jnp.float32)
    weight = jnp.zeros((rows, 256), jnp.float32)
    for k in range(routes.shape[1]):
        hit = routes[:, k:k + 1] == named
        chosen = jnp.where(hit, 1.0, chosen)
        weight = jnp.where(hit, gates[:, k:k + 1], weight)
    lower = (lax.broadcasted_iota(jnp.int32, (rows, rows), 0) >= lax.broadcasted_iota(jnp.int32, (rows, rows), 1))
    lower = jnp.where(lower, 1.0, 0.0).astype(jnp.bfloat16)
    count = jnp.dot(lower, chosen.astype(jnp.bfloat16), preferred_element_type=jnp.float32)
    match = jnp.where((chosen > 0.5) & (count == (slot + 1).astype(jnp.float32)), 1.0, 0.0)
    wfull = weight * match
    whigh = wfull.astype(jnp.bfloat16)
    wmat[0] = whigh
    wmat[1] = (wfull - whigh.astype(jnp.float32)).astype(jnp.bfloat16)
    pick = match.T.astype(jnp.bfloat16)[:4 * CAP]

    small[2].wait()
    for r in (1, 2, 3):
        pass
    for piece in range(0, quarter, 512):
        vals = []
        for q in range(2):
            col = pl.multiple_of(c * 2 * quarter + q * quarter + piece, 128)
            vals.append(jnp.dot(pick, tok[:, pl.ds(col, 512)], preferred_element_type=jnp.float32))
        for r in (1, 2, 3):
            both = jnp.concatenate([v[r * CAP:(r + 1) * CAP] for v in vals], axis=0)
            sbuf[r - 1, :, piece:piece + 512] = both.astype(jnp.bfloat16)
    pl.semaphore_wait(barrier, 4 + (z > 0).astype(jnp.int32) + (z < chips - 1).astype(jnp.int32))
    sends = []
    for r in (1, 2, 3):
        copy = pltpu.make_async_remote_copy(
            src_ref=sbuf.at[r - 1], dst_ref=xr.at[c, r - 1], send_sem=ds_send.at[r - 1],
            recv_sem=ds_recv.at[r - 1], device_id=(rel[r], t), device_id_type=MESH)
        copy.start()
        sends.append(copy)
    own = jnp.concatenate([pick[:CAP].astype(jnp.float32), jnp.zeros((8, rows), jnp.float32)], axis=0).astype(jnp.bfloat16)
    for col in range(0, depth, 512):
        xa[:, col:col + 512] = jnp.dot(own, tok[:, col:col + 512], preferred_element_type=jnp.float32).astype(jnp.bfloat16)

    forwards = []

    def forward(r):
        sends[r - 1].wait_recv()
        copy = pltpu.make_async_remote_copy(
            src_ref=xr.at[c, r - 1], dst_ref=xr.at[c, r - 1], send_sem=fw_send.at[r - 1],
            recv_sem=fw_recv.at[r - 1], device_id=(me, sib), device_id_type=MESH)
        copy.start()
        forwards.append(copy)

    def sibling_in(r):
        pltpu.make_async_remote_copy(
            src_ref=xr.at[1 - c, r - 1], dst_ref=xr.at[1 - c, r - 1], send_sem=fw_send.at[r - 1],
            recv_sem=fw_recv.at[r - 1], device_id=(me, sib), device_id_type=MESH).wait_recv()

    def unpack(half, q, r, piece):
        return xr[half, r - 1, :, piece:piece + 512].astype(jnp.float32)[q * CAP:(q + 1) * CAP]

    groups = [(0, 512), (512, 512), (1024, pad_units - 1024)]
    pieces = [(p, g) for p in range(3) for g in range(3)]
    n_pieces = len(pieces)

    def window(shard, n):
        p, g = pieces[n]
        return hid.at[shard, pl.ds(CUTS[p], CUTS[p + 1] - CUTS[p]), pl.ds(groups[g][0], groups[g][1])]

    def hop(shard, n, sem, dev):
        return pltpu.make_async_remote_copy(
            src_ref=window(shard, n), dst_ref=window(shard, n), send_sem=sem,
            recv_sem=ag_recv.at[shard, n], device_id=(me, dev), device_id_type=MESH)

    def push(shard, dist, n, do_up, do_dn):
        if do_up:
            @pl.when(z < chips - 1)
            def _():
                hop(shard, n, up_send.at[dist, n], t + 2).start()
        if do_dn:
            @pl.when(z > 0)
            def _():
                hop(shard, n, dn_send.at[dist, n], t - 2).start()

    def drain(shard, dist, n, do_up, do_dn):
        if do_up:
            @pl.when(z < chips - 1)
            def _():
                hop(shard, n, up_send.at[dist, n], t + 2).wait_send()
        if do_dn:
            @pl.when(z > 0)
            def _():
                hop(shard, n, dn_send.at[dist, n], t - 2).wait_send()

    def relay(dist, n):
        @pl.when(z >= dist)
        def _():
            shard = t - 2 * dist
            hop(shard, n, up_send.at[dist, n], t).wait_recv()
            push(shard, dist, n, dist < chips - 1, False)
            hop(shard, n, sb_send.at[0, dist, n], sib).start()

        @pl.when(z + dist <= chips - 1)
        def _():
            shard = t + 2 * dist
            hop(shard, n, dn_send.at[dist, n], t).wait_recv()
            push(shard, dist, n, False, dist < chips - 1)
            hop(shard, n, sb_send.at[1, dist, n], sib).start()

    xs = (xa, xb, xc)

    def compute(p, g):
        start, size = groups[g]
        for col in range(start, start + size, CHUNK):
            width = min(CHUNK, start + size - col)
            if p == 0:
                for copy in loads[col // CHUNK]:
                    copy.wait()
            left = xs[p][...]
            ga = contract_last(left, wg[col:col + width, :])
            ua = contract_last(left, wu[col:col + width, :])
            h = ga / (1.0 + jnp.exp(-ga)) * ua
            if p == 0:
                full = h[:32]
                carry[0, :, col:col + width] = h[32:40]
            elif p == 1:
                full = jnp.concatenate([carry[0, :, col:col + width], h[:72]], axis=0)
                carry[1, :, col:col + width] = h[72:80]
            else:
                full = jnp.concatenate([carry[1, :, col:col + width], h[:40]], axis=0)
            hid[t, CUTS[p]:CUTS[p + 1], col:col + width] = full.astype(jnp.bfloat16)

    def stage(n):
        if n < n_pieces:
            p, g = pieces[n]
            if g == 0 and p == 1:
                sibling_in(1)
                sibling_in(2)
                for half in range(2):
                    for q in range(2):
                        for piece in range(0, quarter, 512):
                            col = half * 2 * quarter + q * quarter + piece
                            both = jnp.concatenate([unpack(half, q, 1, piece), unpack(half, q, 2, piece)], axis=0)
                            xb[:, col:col + 512] = both.astype(jnp.bfloat16)
            if g == 0 and p == 2:
                sibling_in(3)
                for half in range(2):
                    for q in range(2):
                        for piece in range(0, quarter, 512):
                            col = half * 2 * quarter + q * quarter + piece
                            both = jnp.concatenate([unpack(half, q, 3, piece), jnp.zeros((8, 512), jnp.float32)], axis=0)
                            xc[:, col:col + 512] = both.astype(jnp.bfloat16)
            compute(p, g)
            push(t, 0, n, True, True)
            hop(t, n, sb_send.at[0, 0, n], sib).start()
            if (p, g) == (0, 2):
                forward(1)
                forward(2)
            if (p, g) == (1, 1):
                forward(3)
        for dist in (1, 2, 3):
            if 0 <= n - dist < n_pieces:
                relay(dist, n - dist)

    for n in range(n_pieces):
        stage(n)

    def down(src, first):
        for q in range(2):
            shard = src * 2 + q

            @pl.when(q != c)
            def _():
                for n in range(n_pieces):
                    hop(shard, n, sb_send.at[0, 0, n], sib).wait_recv()
            off = pl.multiple_of(src * 2 * units + q * (units - half_pad), 128)
            for col in range(0, feats, CHUNK):
                part = contract_last(hid[shard], wd[col:col + CHUNK, pl.ds(off, pad_units)])
                if first and q == 0:
                    acc[:, col:col + CHUNK] = part
                else:
                    acc[:, col:col + CHUNK] += part

    wd_load.wait()
    down(z, True)
    low = 1 - z // 2
    for k in (1, 2, 3):
        stage(n_pieces + k - 1)
        up_src = k - (k <= z).astype(jnp.int32)
        dn_src = 3 - (k - (k <= 3 - z).astype(jnp.int32))
        down(low * up_src + (1 - low) * dn_src, False)

    half_f = feats // 2
    back = []
    for r in (3, 1, 2, 0):
        block = acc[r * CAP:(r + 1) * CAP, :]
        packed = jnp.concatenate([block[:, :half_f], block[:, half_f:]], axis=0).astype(jnp.bfloat16)
        if r == 0:
            ret[0] = packed
        else:
            pbuf[r - 1] = packed
            copy = pltpu.make_async_remote_copy(
                src_ref=pbuf.at[r - 1], dst_ref=ret.at[r], send_sem=rt_send.at[r - 1],
                recv_sem=rt_recv.at[r - 1], device_id=(rel[r], t), device_id_type=MESH)
            copy.start()
            back.append(copy)
    for copy in sends + forwards:
        copy.wait_send()
    for n in range(n_pieces):
        drain(t, 0, n, True, True)
        hop(t, n, sb_send.at[0, 0, n], sib).wait_send()
        for dist in (1, 2, 3):
            @pl.when(z >= dist)
            def _():
                drain(t - 2 * dist, dist, n, dist < chips - 1, False)
                hop(t - 2 * dist, n, sb_send.at[0, dist, n], sib).wait_send()

            @pl.when(z + dist <= chips - 1)
            def _():
                drain(t + 2 * dist, dist, n, False, dist < chips - 1)
                hop(t + 2 * dist, n, sb_send.at[1, dist, n], sib).wait_send()
    for copy in back:
        copy.wait()
    blocks = [ret[r].astype(jnp.float32) for r in range(4)]
    zero = jnp.zeros((256 - 4 * CAP, half_f), jnp.float32)
    for q in range(2):
        stack = jnp.concatenate([b[q * CAP:(q + 1) * CAP] for b in blocks] + [zero], axis=0).astype(jnp.bfloat16)
        total = jnp.dot(wmat[0], stack, preferred_element_type=jnp.float32)
        total += jnp.dot(wmat[1], stack, preferred_element_type=jnp.float32)
        out_ref[:, q * half_f:(q + 1) * half_f] = total.astype(jnp.bfloat16)


def fast_body(tokens, routes, gates, gate_proj, up_proj, down_proj):
    rows, depth = tokens.shape
    units = gate_proj.shape[1]
    feats = down_proj.shape[1]
    pad_units = -(-units // 128) * 128
    bf = jnp.bfloat16
    dma = pltpu.SemaphoreType.DMA
    spans = -(-units // CHUNK)
    any_spec = pl.BlockSpec(memory_space=pl.ANY)
    return pl.pallas_call(
        functools.partial(kernel, (depth, units, feats, rows)),
        out_shape=jax.ShapeDtypeStruct((rows, feats), bf),
        in_specs=[any_spec] * 6,
        out_specs=pl.BlockSpec(memory_space=pltpu.VMEM),
        scratch_shapes=[
            pltpu.VMEM((rows, depth), bf),
            pltpu.VMEM(routes.shape, jnp.int32),
            pltpu.VMEM(gates.shape, jnp.float32),
            pltpu.VMEM((pad_units, depth), bf),
            pltpu.VMEM((pad_units, depth), bf),
            pltpu.VMEM((feats, down_proj.shape[2]), bf),
            pltpu.VMEM((3, 2 * CAP, depth // 4), bf),
            pltpu.VMEM((2, 3, 2 * CAP, depth // 4), bf),
            pltpu.VMEM((48, depth), bf),
            pltpu.VMEM((80, depth), bf),
            pltpu.VMEM((48, depth), bf),
            pltpu.VMEM((8, 4 * CAP, pad_units), bf),
            pltpu.VMEM((2, 8, pad_units), jnp.float32),
            pltpu.VMEM((4 * CAP, feats), jnp.float32),
            pltpu.VMEM((3, 2 * CAP, feats // 2), bf),
            pltpu.VMEM((4, 2 * CAP, feats // 2), bf),
            pltpu.VMEM((2, rows, 256), bf),
            dma((3,)), dma((2, spans)), dma,
            dma((3,)), dma((3,)), dma((3,)), dma((3,)),
            dma((4, 9)), dma((4, 9)), dma((2, 4, 9)), dma((8, 9)),
            dma((3,)), dma((3,)),
        ],
        compiler_params=pltpu.CompilerParams(
            collective_id=0, has_side_effects=True, vmem_limit_bytes=67000000),
        cost_estimate=pl.CostEstimate(
            flops=2 * 4 * CAP * 3 * units * depth, transcendentals=4 * CAP * units,
            bytes_accessed=3 * 2 * units * depth),
        name="moe_step",
    )(tokens, routes, gates, gate_proj, up_proj, down_proj)


def tiles(mesh):
    return mesh.shape["expert"] == WIN and mesh.shape["tensor"] == 8


def solution(mesh):
    in_specs = (
        P("expert", None),
        P("expert", None),
        P("expert", None),
        P("expert", "tensor", None),
        P("expert", "tensor", None),
        P("expert", "tensor", None),
    )
    out_specs = P("expert", "tensor")
    body = fast_body if tiles(mesh) else plain_body
    return jax.shard_map(body, mesh=mesh, in_specs=in_specs, out_specs=out_specs, check_vma=False)
```

```python
import functools
import jax
import jax.numpy as jnp
from jax import lax
from jax.experimental import pallas as pl
from jax.experimental.pallas import tpu as pltpu
from jax.sharding import PartitionSpec as P

WIN = 4
CAP = 40
MESH = pl.DeviceIdType.MESH


def slot_tables(route_block, gate_block):
    row_count = route_block.shape[0]
    experts = jnp.arange(WIN, dtype=jnp.int32)
    hits = route_block[None, :, :] == experts[:, None, None]
    chosen = jnp.any(hits, axis=2)
    position = jnp.cumsum(chosen.astype(jnp.int32), axis=1) - 1
    slots = jnp.arange(CAP, dtype=jnp.int32)
    match = chosen[:, None, :] & (position[:, None, :] == slots[None, :, None])
    row_ids = jnp.arange(row_count, dtype=jnp.int32)
    row_index = jnp.sum(jnp.where(match, row_ids[None, None, :], 0), axis=2)
    filled = jnp.any(match, axis=2)
    weight = jnp.sum(
        jnp.where(hits, gate_block[None, :, :], jnp.zeros((), gate_block.dtype)), axis=2
    )
    return (position, row_index, filled, weight)


def contract_last(left, right):
    return lax.dot_general(
        left, right, (((1,), (1,)), ((), ())), preferred_element_type=jnp.float32
    )


def plain_body(tokens, routes, gates, gate_proj, up_proj, down_proj):
    groups = lax.axis_size("expert")
    split = groups // WIN
    width = tokens.shape[1]
    w_gate = gate_proj[0]
    w_up = up_proj[0]
    w_down = down_proj[0]
    position, row_index, filled, weight = slot_tables(routes, gates)
    picked = jnp.take(tokens, row_index, axis=0)
    picked = jnp.where(filled[:, :, None], picked, jnp.zeros((), tokens.dtype))
    outgoing = jnp.repeat(picked, split, axis=0)
    slot_rows = groups * CAP
    arrived = lax.all_to_all(outgoing, "expert", split_axis=0, concat_axis=0, tiled=True)
    flat_rows = arrived.reshape(slot_rows, width)
    gate_act = contract_last(flat_rows, w_gate)
    up_act = contract_last(flat_rows, w_up)
    hidden = (jax.nn.silu(gate_act) * up_act).astype(jnp.bfloat16)
    partial_value = contract_last(lax.all_gather(hidden, "tensor", axis=1, tiled=True), w_down)
    partial_value = partial_value.astype(jnp.bfloat16).reshape(groups, CAP, w_down.shape[0])
    returned = lax.all_to_all(partial_value, "expert", split_axis=0, concat_axis=0, tiled=True)
    expert_out = returned.astype(jnp.float32).reshape(WIN, split, CAP, w_down.shape[0]).sum(axis=1)
    flat_sum = expert_out.reshape(WIN * CAP, w_down.shape[0])
    offsets = jnp.arange(WIN, dtype=jnp.int32)[:, None] * CAP
    index = offsets + jnp.clip(position, 0, CAP - 1)
    values = jnp.take(flat_sum, index, axis=0)
    return jnp.sum(values * weight[:, :, None], axis=0).astype(jnp.bfloat16)


CUTS = (0, 32, 112, 160)
CHUNK = 256


def kernel(cfg, tok_h, rou_h, gat_h, wg_h, wu_h, wd_h, out_ref,
           tok, rou, gat, flip, wg, wu, wd, sbuf, xr, xa, xb, xc, hid, turn, carry, acc, pbuf, ret, wmat,
           in_sem, w_sem, d_sem, ds_send, ds_recv, fw_send, fw_recv,
           up_send, dn_send, sb_send, ag_recv, rt_send, rt_recv):
    depth, units, feats, rows = cfg
    chips = 4
    quarter = depth // 4
    pad_units = wg.shape[0]
    half_pad = pad_units - units
    me = lax.axis_index("expert")
    t = lax.axis_index("tensor")
    z = t // 2
    c = t % 2
    x = me % 2
    y = me // 2
    sib = t + 1 - 2 * c
    rel = [me, y * 2 + (1 - x), (1 - y) * 2 + x, (1 - y) * 2 + (1 - x)]

    small = [pltpu.make_async_copy(rou_h, rou, in_sem.at[0]),
             pltpu.make_async_copy(gat_h, gat, in_sem.at[1]),
             pltpu.make_async_copy(tok_h, tok, in_sem.at[2])]
    for copy in small:
        copy.start()
    spans = [(k, min(CHUNK, units - k)) for k in range(0, units, CHUNK)]
    loads = []
    for k, (start, size) in enumerate(spans):
        dst = pl.multiple_of(start + half_pad * c, half_pad)
        loads.append([
            pltpu.make_async_copy(wg_h.at[0, pl.ds(start, size), :], wg.at[pl.ds(dst, size), :], w_sem.at[0, k]),
            pltpu.make_async_copy(wu_h.at[0, pl.ds(start, size), :], wu.at[pl.ds(dst, size), :], w_sem.at[1, k])])
    for pair in loads:
        for copy in pair:
            copy.start()
    wd_load = pltpu.make_async_copy(wd_h.at[0], wd, d_sem)
    wd_load.start()
    gap = pl.multiple_of((1 - c) * units, half_pad)
    wg[pl.ds(gap, half_pad), :] = jnp.zeros((half_pad, depth), wg.dtype)
    wu[pl.ds(gap, half_pad), :] = jnp.zeros((half_pad, depth), wu.dtype)

    barrier = pltpu.get_barrier_semaphore()
    for r in (1, 2, 3):
        pl.semaphore_signal(barrier, inc=1, device_id=(rel[r], t), device_id_type=MESH)
    pl.semaphore_signal(barrier, inc=1, device_id=(me, sib), device_id_type=MESH)

    @pl.when(z < chips - 1)
    def _():
        pl.semaphore_signal(barrier, inc=1, device_id=(me, t + 2), device_id_type=MESH)

    @pl.when(z > 0)
    def _():
        pl.semaphore_signal(barrier, inc=1, device_id=(me, t - 2), device_id_type=MESH)

    small[0].wait()
    small[1].wait()
    lane = lax.broadcasted_iota(jnp.int32, (rows, 256), 1)
    group = (lane >= CAP).astype(jnp.int32) + (lane >= 2 * CAP).astype(jnp.int32) + (lane >= 3 * CAP).astype(jnp.int32)
    named = jnp.where(group == 0, rel[0], jnp.where(group == 1, rel[1], jnp.where(group == 2, rel[2], rel[3])))
    named = jnp.where(lane >= 4 * CAP, -1, named)
    slot = lane - CAP * group
    top = rou.shape[0]
    flip[...] = jnp.zeros_like(flip)
    flip[0:top, :] = rou[...].astype(jnp.float32)
    flip[top:2 * top, :] = gat[...]
    columns = flip[...].T
    named = named.astype(jnp.float32)
    chosen = jnp.zeros((rows, 256), jnp.float32)
    weight = jnp.zeros((rows, 256), jnp.float32)
    for k in range(top):
        hit = columns[:, k:k + 1] == named
        chosen = jnp.where(hit, 1.0, chosen)
        weight = jnp.where(hit, columns[:, top + k:top + k + 1], weight)
    lower = (lax.broadcasted_iota(jnp.int32, (rows, rows), 0) >= lax.broadcasted_iota(jnp.int32, (rows, rows), 1))
    lower = jnp.where(lower, 1.0, 0.0).astype(jnp.bfloat16)
    count = jnp.dot(lower, chosen.astype(jnp.bfloat16), preferred_element_type=jnp.float32)
    match = jnp.where((chosen > 0.5) & (count == (slot + 1).astype(jnp.float32)), 1.0, 0.0)
    wfull = weight * match
    whigh = wfull.astype(jnp.bfloat16)
    wmat[0] = whigh
    wmat[1] = (wfull - whigh.astype(jnp.float32)).astype(jnp.bfloat16)
    pick = match.T.astype(jnp.bfloat16)[:4 * CAP]

    small[2].wait()
    for piece in range(0, quarter, 512):
        vals = []
        for q in range(2):
            col = pl.multiple_of(c * 2 * quarter + q * quarter + piece, 128)
            vals.append(jnp.dot(pick, tok[:, pl.ds(col, 512)], preferred_element_type=jnp.float32))
        for r in (1, 2, 3):
            both = jnp.concatenate([v[r * CAP:(r + 1) * CAP] for v in vals], axis=0)
            sbuf[r - 1, :, piece:piece + 512] = both.astype(jnp.bfloat16)
    pl.semaphore_wait(barrier, 4 + (z > 0).astype(jnp.int32) + (z < chips - 1).astype(jnp.int32))
    sends = []
    for r in (1, 2, 3):
        copy = pltpu.make_async_remote_copy(
            src_ref=sbuf.at[r - 1], dst_ref=xr.at[c, r - 1], send_sem=ds_send.at[r - 1],
            recv_sem=ds_recv.at[r - 1], device_id=(rel[r], t), device_id_type=MESH)
        copy.start()
        sends.append(copy)
    own = jnp.concatenate([pick[:CAP].astype(jnp.float32), jnp.zeros((8, rows), jnp.float32)], axis=0).astype(jnp.bfloat16)
    for col in range(0, depth, 512):
        xa[:, col:col + 512] = jnp.dot(own, tok[:, col:col + 512], preferred_element_type=jnp.float32).astype(jnp.bfloat16)

    forwards = []

    def forward(r):
        sends[r - 1].wait_recv()
        copy = pltpu.make_async_remote_copy(
            src_ref=xr.at[c, r - 1], dst_ref=xr.at[c, r - 1], send_sem=fw_send.at[r - 1],
            recv_sem=fw_recv.at[r - 1], device_id=(me, sib), device_id_type=MESH)
        copy.start()
        forwards.append(copy)

    def sibling_in(r):
        pltpu.make_async_remote_copy(
            src_ref=xr.at[1 - c, r - 1], dst_ref=xr.at[1 - c, r - 1], send_sem=fw_send.at[r - 1],
            recv_sem=fw_recv.at[r - 1], device_id=(me, sib), device_id_type=MESH).wait_recv()

    def unpack(half, q, r, piece):
        return xr[half, r - 1, :, piece:piece + 512].astype(jnp.float32)[q * CAP:(q + 1) * CAP]

    groups = [(0, 512), (512, 512), (1024, pad_units - 1024)]
    pieces = [(p, g) for p in range(3) for g in range(3)]
    n_pieces = len(pieces)

    def window(shard, n):
        p, g = pieces[n]
        return hid.at[shard, pl.ds(CUTS[p], CUTS[p + 1] - CUTS[p]), pl.ds(groups[g][0], groups[g][1])]

    def hop(shard, n, sem, dev):
        return pltpu.make_async_remote_copy(
            src_ref=window(shard, n), dst_ref=window(shard, n), send_sem=sem,
            recv_sem=ag_recv.at[shard, n], device_id=(me, dev), device_id_type=MESH)

    def push(shard, dist, n, do_up, do_dn):
        if do_up:
            @pl.when(z < chips - 1)
            def _():
                hop(shard, n, up_send.at[dist, n], t + 2).start()
        if do_dn:
            @pl.when(z > 0)
            def _():
                hop(shard, n, dn_send.at[dist, n], t - 2).start()

    def drain(shard, dist, n, do_up, do_dn):
        if do_up:
            @pl.when(z < chips - 1)
            def _():
                hop(shard, n, up_send.at[dist, n], t + 2).wait_send()
        if do_dn:
            @pl.when(z > 0)
            def _():
                hop(shard, n, dn_send.at[dist, n], t - 2).wait_send()

    def relay(dist, n):
        @pl.when(z >= dist)
        def _():
            shard = t - 2 * dist
            hop(shard, n, up_send.at[dist, n], t).wait_recv()
            push(shard, dist, n, dist < chips - 1, False)
            hop(shard, n, sb_send.at[0, dist, n], sib).start()

        @pl.when(z + dist <= chips - 1)
        def _():
            shard = t + 2 * dist
            hop(shard, n, dn_send.at[dist, n], t).wait_recv()
            push(shard, dist, n, False, dist < chips - 1)
            hop(shard, n, sb_send.at[1, dist, n], sib).start()

    xs = (xa, xb, xc)

    def compute(p, g):
        start, size = groups[g]
        step = CHUNK if p == 0 else 512
        for col in range(start, start + size, step):
            width = min(step, start + size - col)
            if p == 0:
                for copy in loads[col // CHUNK]:
                    copy.wait()
            few = xs[p][...]
            ga = contract_last(wg[col:col + width, :], few)
            ua = contract_last(wu[col:col + width, :], few)
            turn[:width, :few.shape[0]] = ga / (1.0 + jnp.exp(-ga)) * ua
            h = turn[:width, :].T
            if p == 0:
                full = h[:32]
                carry[0, :, col:col + width] = h[32:40]
            elif p == 1:
                full = jnp.concatenate([carry[0, :, col:col + width], h[:72]], axis=0)
                carry[1, :, col:col + width] = h[72:80]
            else:
                full = jnp.concatenate([carry[1, :, col:col + width], h[:40]], axis=0)
            hid[t, CUTS[p]:CUTS[p + 1], col:col + width] = full.astype(jnp.bfloat16)

    def stage(n):
        if n < n_pieces:
            p, g = pieces[n]
            if g == 0 and p == 1:
                sibling_in(1)
                sibling_in(2)
                for half in range(2):
                    for q in range(2):
                        for piece in range(0, quarter, 512):
                            col = half * 2 * quarter + q * quarter + piece
                            both = jnp.concatenate([unpack(half, q, 1, piece), unpack(half, q, 2, piece)], axis=0)
                            xb[:, col:col + 512] = both.astype(jnp.bfloat16)
            if g == 0 and p == 2:
                sibling_in(3)
                for half in range(2):
                    for q in range(2):
                        for piece in range(0, quarter, 512):
                            col = half * 2 * quarter + q * quarter + piece
                            both = jnp.concatenate([unpack(half, q, 3, piece), jnp.zeros((8, 512), jnp.float32)], axis=0)
                            xc[:, col:col + 512] = both.astype(jnp.bfloat16)
            compute(p, g)
            push(t, 0, n, True, True)
            hop(t, n, sb_send.at[0, 0, n], sib).start()
            if (p, g) == (0, 2):
                forward(1)
                forward(2)
            if (p, g) == (1, 1):
                forward(3)
        for dist in (1, 2, 3):
            if 0 <= n - dist < n_pieces:
                relay(dist, n - dist)

    for n in range(n_pieces):
        stage(n)

    def down(src, first):
        for q in range(2):
            shard = src * 2 + q

            @pl.when(q != c)
            def _():
                for n in range(n_pieces):
                    hop(shard, n, sb_send.at[0, 0, n], sib).wait_recv()
            off = pl.multiple_of(src * 2 * units + q * (units - half_pad), 128)
            for col in range(0, feats, CHUNK):
                part = contract_last(wd[col:col + CHUNK, pl.ds(off, pad_units)], hid[shard])
                if first and q == 0:
                    acc[col:col + CHUNK, :4 * CAP] = part
                else:
                    acc[col:col + CHUNK, :4 * CAP] += part

    wd_load.wait()
    down(z, True)
    low = 1 - z // 2
    for k in (1, 2, 3):
        stage(n_pieces + k - 1)
        up_src = k - (k <= z).astype(jnp.int32)
        dn_src = 3 - (k - (k <= 3 - z).astype(jnp.int32))
        down(low * up_src + (1 - low) * dn_src, False)

    half_f = feats // 2
    back = []
    sums = acc[...].T
    for r in (3, 1, 2, 0):
        block = sums[r * CAP:(r + 1) * CAP, :]
        packed = jnp.concatenate([block[:, :half_f], block[:, half_f:]], axis=0).astype(jnp.bfloat16)
        if r == 0:
            ret[0] = packed
        else:
            pbuf[r - 1] = packed
            copy = pltpu.make_async_remote_copy(
                src_ref=pbuf.at[r - 1], dst_ref=ret.at[r], send_sem=rt_send.at[r - 1],
                recv_sem=rt_recv.at[r - 1], device_id=(rel[r], t), device_id_type=MESH)
            copy.start()
            back.append(copy)
    for copy in sends + forwards:
        copy.wait_send()
    for n in range(n_pieces):
        drain(t, 0, n, True, True)
        hop(t, n, sb_send.at[0, 0, n], sib).wait_send()
        for dist in (1, 2, 3):
            @pl.when(z >= dist)
            def _():
                drain(t - 2 * dist, dist, n, dist < chips - 1, False)
                hop(t - 2 * dist, n, sb_send.at[0, dist, n], sib).wait_send()

            @pl.when(z + dist <= chips - 1)
            def _():
                drain(t + 2 * dist, dist, n, False, dist < chips - 1)
                hop(t + 2 * dist, n, sb_send.at[1, dist, n], sib).wait_send()
    for copy in back:
        copy.wait()
    blocks = [ret[r].astype(jnp.float32) for r in range(4)]
    zero = jnp.zeros((256 - 4 * CAP, half_f), jnp.float32)
    for q in range(2):
        stack = jnp.concatenate([b[q * CAP:(q + 1) * CAP] for b in blocks] + [zero], axis=0).astype(jnp.bfloat16)
        total = jnp.dot(wmat[0], stack, preferred_element_type=jnp.float32)
        total += jnp.dot(wmat[1], stack, preferred_element_type=jnp.float32)
        out_ref[:, q * half_f:(q + 1) * half_f] = total.astype(jnp.bfloat16)


def fast_body(tokens, routes, gates, gate_proj, up_proj, down_proj):
    rows, depth = tokens.shape
    units = gate_proj.shape[1]
    feats = down_proj.shape[1]
    pad_units = -(-units // 128) * 128
    bf = jnp.bfloat16
    dma = pltpu.SemaphoreType.DMA
    spans = -(-units // CHUNK)
    any_spec = pl.BlockSpec(memory_space=pl.ANY)
    return pl.pallas_call(
        functools.partial(kernel, (depth, units, feats, rows)),
        out_shape=jax.ShapeDtypeStruct((rows, feats), bf),
        in_specs=[any_spec] * 6,
        out_specs=pl.BlockSpec(memory_space=pltpu.VMEM),
        scratch_shapes=[
            pltpu.VMEM((rows, depth), bf),
            pltpu.VMEM(routes.shape[::-1], jnp.int32),
            pltpu.VMEM(gates.shape[::-1], jnp.float32),
            pltpu.VMEM((128, rows), jnp.float32),
            pltpu.VMEM((pad_units, depth), bf),
            pltpu.VMEM((pad_units, depth), bf),
            pltpu.VMEM((feats, down_proj.shape[2]), bf),
            pltpu.VMEM((3, 2 * CAP, depth // 4), bf),
            pltpu.VMEM((2, 3, 2 * CAP, depth // 4), bf),
            pltpu.VMEM((48, depth), bf),
            pltpu.VMEM((80, depth), bf),
            pltpu.VMEM((48, depth), bf),
            pltpu.VMEM((8, 4 * CAP, pad_units), bf),
            pltpu.VMEM((512, 128), jnp.float32),
            pltpu.VMEM((2, 8, pad_units), jnp.float32),
            pltpu.VMEM((feats, 256), jnp.float32),
            pltpu.VMEM((3, 2 * CAP, feats // 2), bf),
            pltpu.VMEM((4, 2 * CAP, feats // 2), bf),
            pltpu.VMEM((2, rows, 256), bf),
            dma((3,)), dma((2, spans)), dma,
            dma((3,)), dma((3,)), dma((3,)), dma((3,)),
            dma((4, 9)), dma((4, 9)), dma((2, 4, 9)), dma((8, 9)),
            dma((3,)), dma((3,)),
        ],
        compiler_params=pltpu.CompilerParams(
            collective_id=0, has_side_effects=True, vmem_limit_bytes=67000000),
        cost_estimate=pl.CostEstimate(
            flops=2 * 4 * CAP * 3 * units * depth, transcendentals=4 * CAP * units,
            bytes_accessed=3 * 2 * units * depth),
        name="moe_step",
    )(tokens, routes.T, gates.T, gate_proj, up_proj, down_proj)


def tiles(mesh):
    return mesh.shape["expert"] == WIN and mesh.shape["tensor"] == 8


def solution(mesh):
    in_specs = (
        P("expert", None),
        P("expert", None),
        P("expert", None),
        P("expert", "tensor", None),
        P("expert", "tensor", None),
        P("expert", "tensor", None),
    )
    out_specs = P("expert", "tensor")
    body = fast_body if tiles(mesh) else plain_body
    return jax.shard_map(body, mesh=mesh, in_specs=in_specs, out_specs=out_specs, check_vma=False)
```

```python
import functools
import jax
import jax.numpy as jnp
from jax import lax
from jax.experimental import pallas as pl
from jax.experimental.pallas import tpu as pltpu
from jax.sharding import PartitionSpec as P

WIN = 4
CAP = 40
MESH = pl.DeviceIdType.MESH


def slot_tables(route_block, gate_block):
    row_count = route_block.shape[0]
    experts = jnp.arange(WIN, dtype=jnp.int32)
    hits = route_block[None, :, :] == experts[:, None, None]
    chosen = jnp.any(hits, axis=2)
    position = jnp.cumsum(chosen.astype(jnp.int32), axis=1) - 1
    slots = jnp.arange(CAP, dtype=jnp.int32)
    match = chosen[:, None, :] & (position[:, None, :] == slots[None, :, None])
    row_ids = jnp.arange(row_count, dtype=jnp.int32)
    row_index = jnp.sum(jnp.where(match, row_ids[None, None, :], 0), axis=2)
    filled = jnp.any(match, axis=2)
    weight = jnp.sum(
        jnp.where(hits, gate_block[None, :, :], jnp.zeros((), gate_block.dtype)), axis=2
    )
    return (position, row_index, filled, weight)


def contract_last(left, right):
    return lax.dot_general(
        left, right, (((1,), (1,)), ((), ())), preferred_element_type=jnp.float32
    )


def plain_body(tokens, routes, gates, gate_proj, up_proj, down_proj):
    groups = lax.axis_size("expert")
    split = groups // WIN
    width = tokens.shape[1]
    w_gate = gate_proj[0]
    w_up = up_proj[0]
    w_down = down_proj[0]
    position, row_index, filled, weight = slot_tables(routes, gates)
    picked = jnp.take(tokens, row_index, axis=0)
    picked = jnp.where(filled[:, :, None], picked, jnp.zeros((), tokens.dtype))
    outgoing = jnp.repeat(picked, split, axis=0)
    slot_rows = groups * CAP
    arrived = lax.all_to_all(outgoing, "expert", split_axis=0, concat_axis=0, tiled=True)
    flat_rows = arrived.reshape(slot_rows, width)
    gate_act = contract_last(flat_rows, w_gate)
    up_act = contract_last(flat_rows, w_up)
    hidden = (jax.nn.silu(gate_act) * up_act).astype(jnp.bfloat16)
    partial_value = contract_last(lax.all_gather(hidden, "tensor", axis=1, tiled=True), w_down)
    partial_value = partial_value.astype(jnp.bfloat16).reshape(groups, CAP, w_down.shape[0])
    returned = lax.all_to_all(partial_value, "expert", split_axis=0, concat_axis=0, tiled=True)
    expert_out = returned.astype(jnp.float32).reshape(WIN, split, CAP, w_down.shape[0]).sum(axis=1)
    flat_sum = expert_out.reshape(WIN * CAP, w_down.shape[0])
    offsets = jnp.arange(WIN, dtype=jnp.int32)[:, None] * CAP
    index = offsets + jnp.clip(position, 0, CAP - 1)
    values = jnp.take(flat_sum, index, axis=0)
    return jnp.sum(values * weight[:, :, None], axis=0).astype(jnp.bfloat16)


CUTS = (0, 32, 112, 160)
CHUNK = 256


def kernel(cfg, tok_h, rou_h, gat_h, wg_h, wu_h, wd_h, out_ref,
           tok, rou, gat, flip, wg, wu, wd, sbuf, xr, xa, xb, xc, hid, turn, carry, acc, pbuf, ret, wmat,
           in_sem, w_sem, d_sem, ds_send, ds_recv, fw_send, fw_recv,
           up_send, dn_send, sb_send, ag_recv, rt_send, rt_recv):
    depth, units, feats, rows = cfg
    chips = 4
    quarter = depth // 4
    pad_units = wg.shape[0]
    half_pad = pad_units - units
    me = lax.axis_index("expert")
    t = lax.axis_index("tensor")
    z = t // 2
    c = t % 2
    x = me % 2
    y = me // 2
    sib = t + 1 - 2 * c
    rel = [me, y * 2 + (1 - x), (1 - y) * 2 + x, (1 - y) * 2 + (1 - x)]

    small = [pltpu.make_async_copy(rou_h, rou, in_sem.at[0]),
             pltpu.make_async_copy(gat_h, gat, in_sem.at[1]),
             pltpu.make_async_copy(tok_h, tok, in_sem.at[2])]
    for copy in small:
        copy.start()
    spans = [(k, min(CHUNK, units - k)) for k in range(0, units, CHUNK)]
    loads = []
    for k, (start, size) in enumerate(spans):
        dst = pl.multiple_of(start + half_pad * c, half_pad)
        loads.append([
            pltpu.make_async_copy(wg_h.at[0, pl.ds(start, size), :], wg.at[pl.ds(dst, size), :], w_sem.at[0, k]),
            pltpu.make_async_copy(wu_h.at[0, pl.ds(start, size), :], wu.at[pl.ds(dst, size), :], w_sem.at[1, k])])
    for pair in loads:
        for copy in pair:
            copy.start()
    wd_load = pltpu.make_async_copy(wd_h.at[0], wd, d_sem)
    wd_load.start()
    gap = pl.multiple_of((1 - c) * units, half_pad)
    wg[pl.ds(gap, half_pad), :] = jnp.zeros((half_pad, depth), wg.dtype)
    wu[pl.ds(gap, half_pad), :] = jnp.zeros((half_pad, depth), wu.dtype)

    barrier = pltpu.get_barrier_semaphore()
    for r in (1, 2, 3):
        pl.semaphore_signal(barrier, inc=1, device_id=(rel[r], t), device_id_type=MESH)
    pl.semaphore_signal(barrier, inc=1, device_id=(me, sib), device_id_type=MESH)

    @pl.when(z < chips - 1)
    def _():
        pl.semaphore_signal(barrier, inc=1, device_id=(me, t + 2), device_id_type=MESH)

    @pl.when(z > 0)
    def _():
        pl.semaphore_signal(barrier, inc=1, device_id=(me, t - 2), device_id_type=MESH)

    pl.semaphore_signal(barrier, inc=1, device_id=(me, (t + 4) % 8), device_id_type=MESH)

    small[0].wait()
    small[1].wait()
    lane = lax.broadcasted_iota(jnp.int32, (rows, 256), 1)
    group = (lane >= CAP).astype(jnp.int32) + (lane >= 2 * CAP).astype(jnp.int32) + (lane >= 3 * CAP).astype(jnp.int32)
    named = jnp.where(group == 0, rel[0], jnp.where(group == 1, rel[1], jnp.where(group == 2, rel[2], rel[3])))
    named = jnp.where(lane >= 4 * CAP, -1, named)
    slot = lane - CAP * group
    top = rou.shape[0]
    flip[...] = jnp.zeros_like(flip)
    flip[0:top, :] = rou[...].astype(jnp.float32)
    flip[top:2 * top, :] = gat[...]
    columns = flip[...].T
    named = named.astype(jnp.float32)
    chosen = jnp.zeros((rows, 256), jnp.float32)
    weight = jnp.zeros((rows, 256), jnp.float32)
    for k in range(top):
        hit = columns[:, k:k + 1] == named
        chosen = jnp.where(hit, 1.0, chosen)
        weight = jnp.where(hit, columns[:, top + k:top + k + 1], weight)
    lower = (lax.broadcasted_iota(jnp.int32, (rows, rows), 0) >= lax.broadcasted_iota(jnp.int32, (rows, rows), 1))
    lower = jnp.where(lower, 1.0, 0.0).astype(jnp.bfloat16)
    count = jnp.dot(lower, chosen.astype(jnp.bfloat16), preferred_element_type=jnp.float32)
    match = jnp.where((chosen > 0.5) & (count == (slot + 1).astype(jnp.float32)), 1.0, 0.0)
    wfull = weight * match
    whigh = wfull.astype(jnp.bfloat16)
    wmat[0] = whigh
    wmat[1] = (wfull - whigh.astype(jnp.float32)).astype(jnp.bfloat16)
    pick = match.T.astype(jnp.bfloat16)[:4 * CAP]

    small[2].wait()
    for piece in range(0, quarter, 512):
        vals = []
        for q in range(2):
            col = pl.multiple_of(c * 2 * quarter + q * quarter + piece, 128)
            vals.append(jnp.dot(pick, tok[:, pl.ds(col, 512)], preferred_element_type=jnp.float32))
        for r in (1, 2, 3):
            both = jnp.concatenate([v[r * CAP:(r + 1) * CAP] for v in vals], axis=0)
            sbuf[r - 1, :, piece:piece + 512] = both.astype(jnp.bfloat16)
    pl.semaphore_wait(barrier, 5 + (z > 0).astype(jnp.int32) + (z < chips - 1).astype(jnp.int32))
    sends = []
    for r in (1, 2, 3):
        copy = pltpu.make_async_remote_copy(
            src_ref=sbuf.at[r - 1], dst_ref=xr.at[c, r - 1], send_sem=ds_send.at[r - 1],
            recv_sem=ds_recv.at[r - 1], device_id=(rel[r], t), device_id_type=MESH)
        if r < 3:
            copy.start()
        sends.append(copy)
    own = jnp.concatenate([pick[:CAP].astype(jnp.float32), jnp.zeros((8, rows), jnp.float32)], axis=0).astype(jnp.bfloat16)
    for col in range(0, depth, 512):
        xa[:, col:col + 512] = jnp.dot(own, tok[:, col:col + 512], preferred_element_type=jnp.float32).astype(jnp.bfloat16)

    forwards = []

    def forward(r):
        sends[r - 1].wait_recv()
        copy = pltpu.make_async_remote_copy(
            src_ref=xr.at[c, r - 1], dst_ref=xr.at[c, r - 1], send_sem=fw_send.at[r - 1],
            recv_sem=fw_recv.at[r - 1], device_id=(me, sib), device_id_type=MESH)
        copy.start()
        forwards.append(copy)

    def sibling_in(r):
        pltpu.make_async_remote_copy(
            src_ref=xr.at[1 - c, r - 1], dst_ref=xr.at[1 - c, r - 1], send_sem=fw_send.at[r - 1],
            recv_sem=fw_recv.at[r - 1], device_id=(me, sib), device_id_type=MESH).wait_recv()

    def unpack(half, q, r, piece):
        return xr[half, r - 1, :, piece:piece + 512].astype(jnp.float32)[q * CAP:(q + 1) * CAP]

    groups = [(0, 512), (512, 512), (1024, pad_units - 1024)]
    pieces = [(p, g) for p in range(3) for g in range(3)]
    n_pieces = len(pieces)

    def window(shard, n):
        p, g = pieces[n]
        return hid.at[shard, pl.ds(CUTS[p], CUTS[p + 1] - CUTS[p]), pl.ds(groups[g][0], groups[g][1])]

    def hop(shard, n, sem, dev):
        return pltpu.make_async_remote_copy(
            src_ref=window(shard, n), dst_ref=window(shard, n), send_sem=sem,
            recv_sem=ag_recv.at[shard, n], device_id=(me, dev), device_id_type=MESH)

    def own_hops(n):
        return ((z < 2, hop(t, n, up_send.at[1, n], t + 4)), (z >= 2, hop(t, n, dn_send.at[1, n], t - 4)),
                (z < 3, hop(t, n, up_send.at[0, n], t + 2)), (z > 0, hop(t, n, dn_send.at[0, n], t - 2)))

    def relay_hops(n):
        return ((z == 2, hop(t - 4, n, up_send.at[2, n], t + 2)), (z == 1, hop(t + 4, n, dn_send.at[2, n], t - 2)))

    def start_all(hops):
        for cond, copy in hops:
            pl.when(cond)(copy.start)

    def drain_all(hops):
        for cond, copy in hops:
            pl.when(cond)(copy.wait_send)

    def take(dist, n):
        for side, cond, shard in ((0, z >= dist, t - 2 * dist), (1, z + dist <= chips - 1, t + 2 * dist)):
            @pl.when(cond)
            def _():
                hop(shard, n, sb_send.at[side, dist, n], sib).wait_recv()
                if dist == 2:
                    start_all(relay_hops(n)[side:side + 1])
                hop(shard, n, sb_send.at[side, dist, n], sib).start()

    xs = (xa, xb, xc)

    def compute(p, g):
        start, size = groups[g]
        step = CHUNK if p == 0 else 512
        for col in range(start, start + size, step):
            width = min(step, start + size - col)
            if p == 0:
                for copy in loads[col // CHUNK]:
                    copy.wait()
            few = xs[p][...]
            ga = contract_last(wg[col:col + width, :], few)
            ua = contract_last(wu[col:col + width, :], few)
            turn[:width, :few.shape[0]] = ga / (1.0 + jnp.exp(-ga)) * ua
            h = turn[:width, :].T
            if p == 0:
                full = h[:32]
                carry[0, :, col:col + width] = h[32:40]
            elif p == 1:
                full = jnp.concatenate([carry[0, :, col:col + width], h[:72]], axis=0)
                carry[1, :, col:col + width] = h[72:80]
            else:
                full = jnp.concatenate([carry[1, :, col:col + width], h[:40]], axis=0)
            hid[t, CUTS[p]:CUTS[p + 1], col:col + width] = full.astype(jnp.bfloat16)

    def stage(n):
        if n < n_pieces:
            p, g = pieces[n]
            if g == 0 and p == 1:
                sibling_in(1)
                sibling_in(2)
                for half in range(2):
                    for q in range(2):
                        for piece in range(0, quarter, 512):
                            col = half * 2 * quarter + q * quarter + piece
                            both = jnp.concatenate([unpack(half, q, 1, piece), unpack(half, q, 2, piece)], axis=0)
                            xb[:, col:col + 512] = both.astype(jnp.bfloat16)
            if g == 0 and p == 2:
                sibling_in(3)
                for half in range(2):
                    for q in range(2):
                        for piece in range(0, quarter, 512):
                            col = half * 2 * quarter + q * quarter + piece
                            both = jnp.concatenate([unpack(half, q, 3, piece), jnp.zeros((8, 512), jnp.float32)], axis=0)
                            xc[:, col:col + 512] = both.astype(jnp.bfloat16)
            compute(p, g)
            start_all(own_hops(n))
            hop(t, n, sb_send.at[0, 0, n], sib).start()
            if n == 0:
                sends[2].start()
            if n == 1:
                forward(1)
                forward(2)
            if n == 3:
                forward(3)
        for dist, lag in ((2, 2), (1, 2), (3, 4)):
            if n - lag >= 0:
                take(dist, n - lag)

    for n in range(n_pieces):
        stage(n)

    def down(src, first):
        for q in range(2):
            shard = src * 2 + q

            @pl.when(q != c)
            def _():
                for n in range(n_pieces):
                    hop(shard, n, sb_send.at[0, 0, n], sib).wait_recv()
            off = pl.multiple_of(src * 2 * units + q * (units - half_pad), 128)
            for col in range(0, feats, CHUNK):
                part = contract_last(wd[col:col + CHUNK, pl.ds(off, pad_units)], hid[shard])
                if first and q == 0:
                    acc[col:col + CHUNK, :4 * CAP] = part
                else:
                    acc[col:col + CHUNK, :4 * CAP] += part

    wd_load.wait()
    down(z, True)
    low = 1 - z // 2
    rest = ([(2, 7), (1, 7), (3, 5), (2, 8), (1, 8)], [(3, 6), (3, 7)], [(3, 8)])
    for k in (1, 2, 3):
        for dist, n in rest[k - 1]:
            take(dist, n)
        up_src = k - (k <= z).astype(jnp.int32)
        dn_src = 3 - (k - (k <= 3 - z).astype(jnp.int32))
        down(low * up_src + (1 - low) * dn_src, False)

    half_f = feats // 2
    back = []
    sums = acc[...].T
    for r in (3, 1, 2, 0):
        block = sums[r * CAP:(r + 1) * CAP, :]
        packed = jnp.concatenate([block[:, :half_f], block[:, half_f:]], axis=0).astype(jnp.bfloat16)
        if r == 0:
            ret[0] = packed
        else:
            pbuf[r - 1] = packed
            copy = pltpu.make_async_remote_copy(
                src_ref=pbuf.at[r - 1], dst_ref=ret.at[r], send_sem=rt_send.at[r - 1],
                recv_sem=rt_recv.at[r - 1], device_id=(rel[r], t), device_id_type=MESH)
            copy.start()
            back.append(copy)
    for copy in sends + forwards:
        copy.wait_send()
    for n in range(n_pieces):
        drain_all(own_hops(n))
        drain_all(relay_hops(n))
        hop(t, n, sb_send.at[0, 0, n], sib).wait_send()
        for dist in (1, 2, 3):
            drain_all(((z >= dist, hop(t - 2 * dist, n, sb_send.at[0, dist, n], sib)),
                       (z + dist <= chips - 1, hop(t + 2 * dist, n, sb_send.at[1, dist, n], sib))))
    for copy in back:
        copy.wait()
    blocks = [ret[r].astype(jnp.float32) for r in range(4)]
    zero = jnp.zeros((256 - 4 * CAP, half_f), jnp.float32)
    for q in range(2):
        stack = jnp.concatenate([b[q * CAP:(q + 1) * CAP] for b in blocks] + [zero], axis=0).astype(jnp.bfloat16)
        total = jnp.dot(wmat[0], stack, preferred_element_type=jnp.float32)
        total += jnp.dot(wmat[1], stack, preferred_element_type=jnp.float32)
        out_ref[:, q * half_f:(q + 1) * half_f] = total.astype(jnp.bfloat16)


def fast_body(tokens, routes, gates, gate_proj, up_proj, down_proj):
    rows, depth = tokens.shape
    units = gate_proj.shape[1]
    feats = down_proj.shape[1]
    pad_units = -(-units // 128) * 128
    bf = jnp.bfloat16
    dma = pltpu.SemaphoreType.DMA
    spans = -(-units // CHUNK)
    any_spec = pl.BlockSpec(memory_space=pl.ANY)
    return pl.pallas_call(
        functools.partial(kernel, (depth, units, feats, rows)),
        out_shape=jax.ShapeDtypeStruct((rows, feats), bf),
        in_specs=[any_spec] * 6,
        out_specs=pl.BlockSpec(memory_space=pltpu.VMEM),
        scratch_shapes=[
            pltpu.VMEM((rows, depth), bf),
            pltpu.VMEM(routes.shape[::-1], jnp.int32),
            pltpu.VMEM(gates.shape[::-1], jnp.float32),
            pltpu.VMEM((128, rows), jnp.float32),
            pltpu.VMEM((pad_units, depth), bf),
            pltpu.VMEM((pad_units, depth), bf),
            pltpu.VMEM((feats, down_proj.shape[2]), bf),
            pltpu.VMEM((3, 2 * CAP, depth // 4), bf),
            pltpu.VMEM((2, 3, 2 * CAP, depth // 4), bf),
            pltpu.VMEM((48, depth), bf),
            pltpu.VMEM((80, depth), bf),
            pltpu.VMEM((48, depth), bf),
            pltpu.VMEM((8, 4 * CAP, pad_units), bf),
            pltpu.VMEM((512, 128), jnp.float32),
            pltpu.VMEM((2, 8, pad_units), jnp.float32),
            pltpu.VMEM((feats, 256), jnp.float32),
            pltpu.VMEM((3, 2 * CAP, feats // 2), bf),
            pltpu.VMEM((4, 2 * CAP, feats // 2), bf),
            pltpu.VMEM((2, rows, 256), bf),
            dma((3,)), dma((2, spans)), dma,
            dma((3,)), dma((3,)), dma((3,)), dma((3,)),
            dma((4, 9)), dma((4, 9)), dma((2, 4, 9)), dma((8, 9)),
            dma((3,)), dma((3,)),
        ],
        compiler_params=pltpu.CompilerParams(
            collective_id=0, has_side_effects=True, vmem_limit_bytes=67000000),
        cost_estimate=pl.CostEstimate(
            flops=2 * 4 * CAP * 3 * units * depth, transcendentals=4 * CAP * units,
            bytes_accessed=3 * 2 * units * depth),
        name="moe_step",
    )(tokens, routes.T, gates.T, gate_proj, up_proj, down_proj)


def tiles(mesh):
    return mesh.shape["expert"] == WIN and mesh.shape["tensor"] == 8


def solution(mesh):
    in_specs = (
        P("expert", None),
        P("expert", None),
        P("expert", None),
        P("expert", "tensor", None),
        P("expert", "tensor", None),
        P("expert", "tensor", None),
    )
    out_specs = P("expert", "tensor")
    body = fast_body if tiles(mesh) else plain_body
    return jax.shard_map(body, mesh=mesh, in_specs=in_specs, out_specs=out_specs, check_vma=False)
```
